32 devices in a mesh: acq: 4 (over z), tile: 8 (over y, x, core).
Axes of the slice: x: 2, y: 2, z: 4, core: 2. Of those that a mesh axis runs over, the one named last changes fastest.
Arguments:
- slc_stack: bfloat16 [16, 2, 512, 1024], P('acq', None, 'tile'), may hold values from -6 to 6
- pair_list: int32 [48, 2], replicated, may hold values from 0 to 15, as said below
Outputs:
- filtered: float32 [48, 2, 128, 64], P('acq', None, 'tile')
The draws below stay inside these ranges and needn't reach their ends.
Inputs may be any that keep to these rules, and one draw needn't show every extreme that they name: `pair_list`: the reference (first entry) of a pair owned by group g is one of group g's acquisitions, g * 4 to (g + 1) * 4 - 1; the secondary lies in another group. The pairs of one group use at most one secondary acquisition from each other group. No pair appears twice.
All inputs are finite; a program needn't handle non-finite values.
Results may differ from the reference program's by a relative error of at most 0.0003.
Values may be sent and summed in bfloat16 or wider, within the bound.
A program may use at most 128 MiB of HBM per device.

```python
import jax
import jax.numpy as jnp
from jax import lax

ACQ_DEV = 4
PAIRS_DEV = 12
RANGE = 1024
AZ_LOOKS = 4
RG_LOOKS = 16
PATCH = 32
ACQ = 16
LINES = 512
N_ACQ = 4


def draw_pair_list(key, part):
    key = jax.random.fold_in(key, 7)
    others = N_ACQ - 1
    spread = min(others, PAIRS_DEV)
    subkeys = jax.random.split(key, 4)
    owner_keys = jax.random.split(subkeys[0], N_ACQ)
    orders = jax.vmap(lambda single: jax.random.permutation(single, others))(owner_keys)
    slot_ids = jnp.arange(PAIRS_DEV, dtype=jnp.int32) % spread
    layers = jnp.arange(PAIRS_DEV, dtype=jnp.int32) // spread
    owners = jnp.arange(N_ACQ, dtype=jnp.int32)[:, None]
    targets = (owners + 1 + orders[:, slot_ids]) % N_ACQ
    picks = jnp.minimum(jax.random.randint(subkeys[1], (N_ACQ, others), 0, ACQ_DEV), jax.random.randint(subkeys[2], (N_ACQ, others), 0, ACQ_DEV))
    seconds = targets * ACQ_DEV + picks[:, slot_ids]
    offsets = jax.random.randint(subkeys[3], (N_ACQ, others), 0, ACQ_DEV)
    firsts = owners * ACQ_DEV + (layers[None, :] + offsets[:, slot_ids]) % ACQ_DEV
    return jnp.stack([firsts, seconds], axis=-1).reshape(N_ACQ * PAIRS_DEV, 2).astype(jnp.int32)


def block_scale(key, extent, cuts, smallest, top_value):
    level, own = 1.0, jax.random.fold_in(key, 6)
    for position, shards_of in cuts:
        steps = jnp.exp(jax.random.uniform(jax.random.fold_in(own, position), (shards_of,), jnp.float32, smallest / len(cuts), top_value / len(cuts)))
        level = level * jnp.repeat(steps, extent[position] // shards_of).reshape([-1 if axis == position else 1 for axis in range(len(extent))])
    return level


def bell_draw(stream_key, extent, width, reach, pieces=(), kind=jnp.bfloat16):
    gain = block_scale(stream_key, extent, pieces, -0.22, 0.18) if pieces else 1.0
    entries = jax.random.normal(stream_key, extent, jnp.float32) * width * gain
    return jnp.minimum(jnp.maximum(entries, -reach), reach).astype(kind)


def setup_inputs(seed: int = 0) -> dict:
    keys = jax.random.split(jax.random.key(seed), 3)
    return {
        "slc_stack": bell_draw(keys[0], (ACQ, 2, LINES, RANGE), 1.0, 6.0, ((0, 4), (2, 8))),
        "pair_list": draw_pair_list(jax.random.fold_in(keys[2], 71), 0),
    }


def dft_tables(length):
    counter = jnp.arange(length, dtype=jnp.int32)
    product = (counter[:, None] * counter[None, :]) % length
    angles = product.astype(jnp.float32) * (2.0 * jnp.pi / length)
    return jnp.cos(angles), jnp.sin(angles)


def taper_table(length):
    centre = (jnp.arange(length, dtype=jnp.float32) + 0.5) * (jnp.pi / length)
    profile = jnp.sin(centre) ** 2
    return profile[:, None] * profile[None, :]


def left_mult(matrix, blocks):
    return jnp.einsum("jk,...kl->...jl", matrix, blocks, precision=lax.Precision.HIGHEST)


def right_mult(blocks, matrix):
    return jnp.einsum("...jk,kl->...jl", blocks, matrix, precision=lax.Precision.HIGHEST)


def filter_patches(real_part, imag_part):
    length = real_part.shape[-1]
    cosine, sine_table = dft_tables(length)
    first_re = left_mult(cosine, real_part) + left_mult(sine_table, imag_part)
    first_im = left_mult(cosine, imag_part) - left_mult(sine_table, real_part)
    spec_re = right_mult(first_re, cosine) + right_mult(first_im, sine_table)
    spec_im = right_mult(first_im, cosine) - right_mult(first_re, sine_table)
    power_map = spec_re * spec_re + spec_im * spec_im
    smooth_rows = power_map + jnp.roll(power_map, 1, axis=-2) + jnp.roll(power_map, -1, axis=-2)
    smoothed = (smooth_rows + jnp.roll(smooth_rows, 1, axis=-1) + jnp.roll(smooth_rows, -1, axis=-1)) / 9.0
    relative = smoothed / (jnp.mean(smoothed, axis=(-2, -1), keepdims=True) + 1e-6)
    weights = jnp.maximum(relative, 0.1) ** 0.25
    scaled_re = weights * spec_re
    scaled_im = weights * spec_im
    back_re = left_mult(cosine, scaled_re) - left_mult(sine_table, scaled_im)
    back_im = left_mult(cosine, scaled_im) + left_mult(sine_table, scaled_re)
    norm_factor = taper_table(length) / float(length * length)
    final_re = (right_mult(back_re, cosine) - right_mult(back_im, sine_table)) * norm_factor
    final_im = (right_mult(back_im, cosine) + right_mult(back_re, sine_table)) * norm_factor
    return final_re, final_im


def cut_patches(planes, half_patch):
    leading = planes.shape[:-2]
    row_count = planes.shape[-2] // half_patch - 1
    col_count = planes.shape[-1] // half_patch - 1
    blocks = planes.reshape(leading + (row_count + 1, half_patch, col_count + 1, half_patch))
    row_pairs = jnp.concatenate([blocks[..., :-1, :, :, :], blocks[..., 1:, :, :, :]], axis=-3)
    both_dims = jnp.concatenate([row_pairs[..., :-1, :], row_pairs[..., 1:, :]], axis=-1)
    return jnp.swapaxes(both_dims, -3, -2)


def join_columns(patches, half_patch):
    left_half = patches[..., :half_patch]
    right_half = patches[..., half_patch:]
    previous = jnp.concatenate([jnp.zeros_like(right_half[..., :1, :, :]), right_half[..., :-1, :, :]], axis=-3)
    columns = jnp.swapaxes(left_half + previous, -3, -2)
    return columns.reshape(columns.shape[:-2] + (columns.shape[-2] * columns.shape[-1],))


def filter_grid(planes, half_patch):
    blocks = cut_patches(planes, half_patch)
    final_re, final_im = filter_patches(blocks[..., 0, :, :, :, :], blocks[..., 1, :, :, :, :])
    merged = jnp.stack([final_re, final_im], axis=-5)
    columns = join_columns(merged, half_patch)
    return columns[..., :half_patch, :], columns[..., half_patch:, :]


def multilook(reference_slab, second_slab):
    ref_re = reference_slab[0].astype(jnp.float32)
    ref_im = reference_slab[1].astype(jnp.float32)
    sec_re = second_slab[0].astype(jnp.float32)
    sec_im = second_slab[1].astype(jnp.float32)
    stacked = jnp.stack([ref_re * sec_re + ref_im * sec_im, ref_im * sec_re - ref_re * sec_im])
    lines_in = stacked.shape[1]
    samples = stacked.shape[2]
    grouped = stacked.reshape(2, lines_in // AZ_LOOKS, AZ_LOOKS, samples // RG_LOOKS, RG_LOOKS)
    return jnp.mean(grouped, axis=(2, 4))


def reference(slc_stack, pair_list):
    half_patch = PATCH // 2

    def per_pair(pair_row):
        reference_slab = lax.dynamic_index_in_dim(slc_stack, pair_row[0], 0, keepdims=False)
        second_slab = lax.dynamic_index_in_dim(slc_stack, pair_row[1], 0, keepdims=False)
        planes = multilook(reference_slab, second_slab)
        padded = jnp.pad(planes, ((0, 0), (0, half_patch), (0, half_patch)))
        upper_half, lower_half = filter_grid(padded, half_patch)
        earlier = jnp.concatenate([jnp.zeros_like(lower_half[:, :1]), lower_half[:, :-1]], axis=1)
        return (upper_half + earlier).reshape(planes.shape)

    return lax.map(per_pair, pair_list)
```

```python
import functools

import jax
import jax.numpy as jnp
import ml_dtypes
import numpy as np
from jax import lax
from jax.experimental import pallas as pl
from jax.experimental.pallas import tpu as pltpu
from jax.sharding import PartitionSpec as P

AZ_LOOKS = 4
RG_LOOKS = 16
PATCH = 32
HALF = PATCH // 2
CHUNKS = 4
MESH = pl.DeviceIdType.MESH
BF16 = jnp.bfloat16
F32 = jnp.float32


def halves(matrix):
    high = matrix.astype(ml_dtypes.bfloat16)
    low = (matrix - high.astype(np.float64)).astype(ml_dtypes.bfloat16)
    return high, low


def tables(width):
    patches = width // HALF
    index = np.arange(PATCH)
    angle = 2.0 * np.pi * ((index[:, None] * index[None, :]) % PATCH) / PATCH
    cos, sin = np.cos(angle), np.sin(angle)
    taper = np.sin(np.pi * (index + 0.5) / PATCH) ** 2
    span = patches * PATCH
    forward = np.zeros((2 * width, 2 * span))
    backward = np.zeros((2 * span, 2 * width))
    for c in range(patches):
        for j in range(PATCH):
            n = c * HALF + j
            if n >= width:
                continue
            at = slice(c * PATCH, (c + 1) * PATCH)
            im = slice(span + c * PATCH, span + (c + 1) * PATCH)
            forward[n, at] = cos[j]
            forward[n, im] = -sin[j]
            forward[width + n, at] = sin[j]
            forward[width + n, im] = cos[j]
            backward[at, n] = cos[:, j] * taper[j]
            backward[im, n] = -sin[:, j] * taper[j]
            backward[at, width + n] = sin[:, j] * taper[j]
            backward[im, width + n] = cos[:, j] * taper[j]
    lines = np.block([[cos, sin], [-sin, cos]])
    scale = taper / float(PATCH * PATCH)
    inverse = np.block([[cos, -sin], [sin, cos]]) * np.concatenate([scale, scale])[:, None]
    upper = np.concatenate([inverse[:HALF], inverse[PATCH : PATCH + HALF]])
    lower = np.concatenate([inverse[HALF:PATCH], inverse[PATCH + HALF :]])
    inverse = np.concatenate([upper, lower], axis=1)
    ring = np.zeros((PATCH, PATCH))
    for k in range(PATCH):
        for step in (-1, 0, 1):
            ring[(k + step) % PATCH, k] = 1.0
    eye = np.eye(patches)
    smooth = np.concatenate([np.kron(eye, ring), np.kron(eye, np.ones((PATCH, PATCH)))], axis=1)

    fh, fl = halves(forward)
    lh, ll = halves(lines)
    ih, il = halves(inverse)
    bh, bl = halves(backward)
    sh = smooth.astype(ml_dtypes.bfloat16)
    return (
        np.concatenate([fh, fh, fl], axis=0),
        np.concatenate([lh, lh, ll], axis=1),
        np.concatenate([ih, ih, il], axis=1),
        np.concatenate([bh, bh, bl], axis=0),
        np.concatenate([sh, sh], axis=0),
    )


def line_order(lines):
    looks = lines // AZ_LOOKS
    order = np.zeros((lines, lines))
    for l in range(AZ_LOOKS):
        for look in range(looks):
            order[l * looks + look, look * AZ_LOOKS + l] = 1.0
    return order.astype(ml_dtypes.bfloat16)


def split(x):
    high = x.astype(BF16)
    return high, (x - high.astype(F32)).astype(BF16)


def mm(a, b):
    return jnp.dot(a, b, preferred_element_type=F32)


def kernel(
    groups, tiles, held, per_owner,
    pairs_ref, slc_ref, order_ref, fwd_ref, lines_ref, inv_ref, bwd_ref, smooth_ref,
    out_ref,
    own, stage, got, looks_w, planes, halo, result,
    send_sem, recv_sem, halo_send, halo_recv,
):
    me = lax.axis_index("acq")
    tile = lax.axis_index("tile")
    lines = slc_ref.shape[2]
    samples = slc_ref.shape[3]
    looks = lines // AZ_LOOKS
    width = samples // RG_LOOKS
    part = samples // CHUNKS
    span = (width // HALF) * PATCH
    left = lax.rem(tile + tiles - 1, tiles)
    right = lax.rem(tile + 1, tiles)

    barrier = pltpu.get_barrier_semaphore()
    for d in range(1, groups):
        pl.semaphore_signal(
            barrier, inc=1, device_id=(lax.rem(me + d, groups), tile), device_id_type=MESH
        )
    for other in (left, right):
        pl.semaphore_signal(barrier, inc=1, device_id=(me, other), device_id_type=MESH)

    for a in range(held):
        for plane in range(2):
            own[a, plane] = mm(order_ref[...], slc_ref[a, plane]).astype(BF16)

    distances = sorted(range(1, groups), key=lambda d: (abs(2 * d - groups), d))

    for d in distances:
        owner = lax.rem(me + d, groups)
        want = jnp.int32(0)
        for p in range(per_owner):
            second = pairs_ref[owner * per_owner + p, 1]
            inside = second - me * held
            want = jnp.where((inside >= 0) & (inside < held), inside, want)
        for q in range(CHUNKS):
            stage[d - 1, q] = own[want, :, :, q * part : (q + 1) * part]

    pl.semaphore_wait(barrier, groups + 1)

    def slab(d, q):
        return pltpu.make_async_remote_copy(
            src_ref=stage.at[d - 1, q],
            dst_ref=got.at[d - 1, q],
            send_sem=send_sem.at[d - 1, q],
            recv_sem=recv_sem.at[d - 1, q],
            device_id=(lax.rem(me + d, groups), tile),
            device_id_type=MESH,
        )

    for d in distances:
        for q in range(CHUNKS):
            slab(d, q).start()

    for q in range(CHUNKS):
        row = lax.broadcasted_iota(jnp.int32, (2 * part, 2 * width), 0)
        col = lax.broadcasted_iota(jnp.int32, (2 * part, 2 * width), 1)
        plane = jnp.where(row >= part, 1, 0)
        goal = plane * width + q * (part // RG_LOOKS) + (row - plane * part) // RG_LOOKS
        looks_w[q] = jnp.where(goal == col, 1.0 / (AZ_LOOKS * RG_LOOKS), 0.0).astype(BF16)

    def halo_copy(d, side):
        return pltpu.make_async_remote_copy(
            src_ref=planes.at[d - 1],
            dst_ref=halo.at[d - 1, side],
            send_sem=halo_send.at[d - 1, side],
            recv_sem=halo_recv.at[d - 1, side],
            device_id=(me, right if side == 0 else left),
            device_id_type=MESH,
        )

    def multilook(d):
        total = jnp.zeros((held * looks, 2 * width), F32)
        for q in range(CHUNKS):
            slab(d, q).wait_recv()
            at = slice(q * part, (q + 1) * part)
            re = [None] * held
            im = [None] * held
            for l in range(AZ_LOOKS):
                rows = slice(l * looks, (l + 1) * looks)
                br = got[d - 1, q, 0, rows, :].astype(F32)
                bi = got[d - 1, q, 1, rows, :].astype(F32)
                for a in range(held):
                    ar = own[a, 0, rows, at].astype(F32)
                    ai = own[a, 1, rows, at].astype(F32)
                    x = ar * br + ai * bi
                    y = ai * br - ar * bi
                    re[a] = x if l == 0 else re[a] + x
                    im[a] = y if l == 0 else im[a] + y
            both = jnp.concatenate(
                [jnp.concatenate(re, axis=0), jnp.concatenate(im, axis=0)], axis=1
            )
            high, low = split(both)
            total = total + mm(high, looks_w[q]) + mm(low, looks_w[q])
        planes[d - 1] = total

    def columns(x):
        high, low = split(x)
        return mm(jnp.concatenate([high, low, high], axis=1), fwd_ref[...])

    def filter_pairs(d):
        mid = columns(planes[d - 1])
        for side in range(2):
            halo_copy(d, side).wait_recv()
        low_part = columns(halo[d - 1, 0])
        later = jnp.where(tile == tiles - 1, 0.0, halo[d - 1, 1])
        high_part = columns(later)

        def patch(first, second, a):
            rows = slice(a * looks, (a + 1) * looks)
            return jnp.concatenate(
                [first[rows, :span], second[rows, :span], first[rows, span:], second[rows, span:]],
                axis=0,
            )

        blocks = [patch(mid, high_part, a) for a in range(held)]
        blocks += [patch(low_part, mid, a) for a in range(held)]
        high, low = split(jnp.concatenate(blocks, axis=1))
        spec = mm(lines_ref[...], jnp.concatenate([high, low, high], axis=0))
        spec_re, spec_im = spec[:PATCH], spec[PATCH:]
        power = spec_re * spec_re + spec_im * spec_im
        rows3 = power + pltpu.roll(power, 1, 0) + pltpu.roll(power, PATCH - 1, 0)
        stacked = jnp.concatenate(
            [rows3[:, i * span : (i + 1) * span] for i in range(2 * held)], axis=0
        )
        high, low = split(stacked)
        sums = mm(jnp.concatenate([high, low], axis=1), smooth_ref[...])
        weights = []
        for i in range(2 * held):
            block = sums[i * PATCH : (i + 1) * PATCH]
            smoothed = block[:, :span] * (1.0 / 9.0)
            mean = jnp.sum(block[:, span:], axis=0, keepdims=True) * (
                1.0 / (3.0 * PATCH * PATCH)
            )
            relative = smoothed / (mean + 1e-6)
            weight = jnp.sqrt(jnp.sqrt(jnp.maximum(relative, 0.1)))
            if i >= held:
                weight = jnp.where(tile == 0, 0.0, weight)
            weights.append(weight)
        weight = jnp.concatenate(weights, axis=1)
        scaled = jnp.concatenate([weight * spec_re, weight * spec_im], axis=0)
        scaled = jnp.concatenate([scaled[:, : held * span], scaled[:, held * span :]], axis=0)
        high, low = split(scaled)
        back = mm(inv_ref[...], jnp.concatenate([high, low, high], axis=0))
        back = jnp.concatenate(
            [
                jnp.concatenate(
                    [back[:HALF, a * span : (a + 1) * span], back[HALF:, a * span : (a + 1) * span]],
                    axis=1,
                )
                for a in range(held)
            ],
            axis=0,
        )
        high, low = split(back)
        final = mm(jnp.concatenate([high, low, high], axis=1), bwd_ref[...])
        for a in range(held):
            result[(d - 1) * held + a] = final[a * looks : (a + 1) * looks]

    before = None
    for d in distances:
        multilook(d)
        for side in range(2):
            halo_copy(d, side).start()
        if before is not None:
            filter_pairs(before)
        before = d
    filter_pairs(before)

    for p in range(per_owner):
        first = pairs_ref[me * per_owner + p, 0] - me * held
        source = pairs_ref[me * per_owner + p, 1] // held
        slot = lax.rem(me - source + groups, groups) - 1
        at = jnp.clip(slot * held + first, 0, (groups - 1) * held - 1)
        lines_out = result[at]
        out_ref[p, 0] = lines_out[:, :width]
        out_ref[p, 1] = lines_out[:, width:]

    for d in distances:
        for q in range(CHUNKS):
            slab(d, q).wait_send()
        for side in range(2):
            halo_copy(d, side).wait_send()


def per_device(groups, tiles, slc_stack, pair_list):
    held, _, lines, samples = slc_stack.shape
    per_owner = pair_list.shape[0] // groups
    looks, width = lines // AZ_LOOKS, samples // RG_LOOKS
    part = samples // CHUNKS
    others = groups - 1
    vmem = pl.BlockSpec(memory_space=pltpu.VMEM)
    smem = pl.BlockSpec(memory_space=pltpu.SMEM)
    constants = [jnp.asarray(t) for t in (line_order(lines),) + tables(width)]
    return pl.pallas_call(
        functools.partial(kernel, groups, tiles, held, per_owner),
        out_shape=jax.ShapeDtypeStruct((per_owner, 2, looks, width), F32),
        in_specs=[smem, vmem] + [vmem] * len(constants),
        out_specs=vmem,
        scratch_shapes=[
            pltpu.VMEM((held, 2, lines, samples), BF16),
            pltpu.VMEM((others, CHUNKS, 2, lines, part), BF16),
            pltpu.VMEM((others, CHUNKS, 2, lines, part), BF16),
            pltpu.VMEM((CHUNKS, 2 * part, 2 * width), BF16),
            pltpu.VMEM((others, held * looks, 2 * width), F32),
            pltpu.VMEM((others, 2, held * looks, 2 * width), F32),
            pltpu.VMEM((others * held, looks, 2 * width), F32),
            pltpu.SemaphoreType.DMA((others, CHUNKS)),
            pltpu.SemaphoreType.DMA((others, CHUNKS)),
            pltpu.SemaphoreType.DMA((others, 2)),
            pltpu.SemaphoreType.DMA((others, 2)),
        ],
        compiler_params=pltpu.CompilerParams(
            collective_id=0, has_side_effects=True, vmem_limit_bytes=48 * 2**20
        ),
    )(pair_list, slc_stack, *constants)


def solution(mesh):
    groups, tiles = mesh.shape["acq"], mesh.shape["tile"]
    return jax.shard_map(
        functools.partial(per_device, groups, tiles),
        mesh=mesh,
        in_specs=(P("acq", None, "tile", None), P()),
        out_specs=P("acq", None, "tile", None),
        check_vma=False,
    )
```

```python
import functools

import jax
import jax.numpy as jnp
import ml_dtypes
import numpy as np
from jax import lax
from jax.experimental import pallas as pl
from jax.experimental.pallas import tpu as pltpu
from jax.sharding import PartitionSpec as P

AZ_LOOKS = 4
RG_LOOKS = 16
PATCH = 32
HALF = PATCH // 2
CHUNKS = 4
VMEM_LIMIT = 64 * 2**20 - 2**16
MESH = pl.DeviceIdType.MESH
BF16 = jnp.bfloat16
F32 = jnp.float32


def halves(matrix):
    high = matrix.astype(ml_dtypes.bfloat16)
    low = (matrix - high.astype(np.float64)).astype(ml_dtypes.bfloat16)
    return high, low


def tables(width):
    patches = width // HALF
    index = np.arange(PATCH)
    angle = 2.0 * np.pi * ((index[:, None] * index[None, :]) % PATCH) / PATCH
    cos, sin = np.cos(angle), np.sin(angle)
    taper = np.sin(np.pi * (index + 0.5) / PATCH) ** 2
    span = patches * PATCH
    forward = np.zeros((2 * width, 2 * span))
    backward = np.zeros((2 * span, 2 * width))
    for c in range(patches):
        for j in range(PATCH):
            n = c * HALF + j
            if n >= width:
                continue
            at = slice(c * PATCH, (c + 1) * PATCH)
            im = slice(span + c * PATCH, span + (c + 1) * PATCH)
            forward[n, at] = cos[j]
            forward[n, im] = -sin[j]
            forward[width + n, at] = sin[j]
            forward[width + n, im] = cos[j]
            backward[at, n] = cos[:, j] * taper[j]
            backward[im, n] = -sin[:, j] * taper[j]
            backward[at, width + n] = sin[:, j] * taper[j]
            backward[im, width + n] = cos[:, j] * taper[j]
    lines = np.block([[cos, sin], [-sin, cos]])
    scale = taper / float(PATCH * PATCH)
    inverse = np.block([[cos, -sin], [sin, cos]]) * np.concatenate([scale, scale])[:, None]
    upper = np.concatenate([inverse[:HALF], inverse[PATCH : PATCH + HALF]])
    lower = np.concatenate([inverse[HALF:PATCH], inverse[PATCH + HALF :]])
    inverse = np.concatenate([upper, lower], axis=1)
    ring = np.zeros((PATCH, PATCH))
    for k in range(PATCH):
        for step in (-1, 0, 1):
            ring[(k + step) % PATCH, k] = 1.0
    eye = np.eye(patches)
    smooth = np.concatenate([np.kron(eye, ring), np.kron(eye, np.ones((PATCH, PATCH)))], axis=1)

    fh, fl = halves(forward)
    lh, ll = halves(lines)
    ih, il = halves(inverse)
    bh, bl = halves(backward)
    sh = smooth.astype(ml_dtypes.bfloat16)
    return (
        np.concatenate([fh, fh, fl], axis=0),
        np.concatenate([lh, lh, ll], axis=1),
        np.concatenate([ih, ih, il], axis=1),
        np.concatenate([bh, bh, bl], axis=0),
        np.concatenate([sh, sh], axis=0),
    )


def line_order(lines):
    looks = lines // AZ_LOOKS
    order = np.zeros((lines, lines))
    for l in range(AZ_LOOKS):
        for look in range(looks):
            order[l * looks + look, look * AZ_LOOKS + l] = 1.0
    return order.astype(ml_dtypes.bfloat16)


def split(x):
    high = x.astype(BF16)
    return high, (x - high.astype(F32)).astype(BF16)


def mm(a, b):
    return jnp.dot(a, b, preferred_element_type=F32)


def kernel(
    groups, tiles, held, per_owner, operands,
    *refs,
):
    inputs, (out_ref,), held_in = refs[:operands], refs[operands : operands + 1], refs[operands + 1 :]
    copied, rest = held_in[:operands], held_in[operands:]
    pairs_ref, slc_ref, order_ref, fwd_ref, lines_ref, inv_ref, bwd_ref, smooth_ref = copied
    (own, stage, got, looks_w, planes, halo, result,
     load_sem, send_sem, recv_sem, halo_send, halo_recv) = rest
    me = lax.axis_index("acq")
    tile = lax.axis_index("tile")
    lines = slc_ref.shape[2]
    samples = slc_ref.shape[3]
    looks = lines // AZ_LOOKS
    width = samples // RG_LOOKS
    part = samples // CHUNKS
    span = (width // HALF) * PATCH
    left = lax.rem(tile + tiles - 1, tiles)
    right = lax.rem(tile + 1, tiles)

    loads = [
        pltpu.make_async_copy(source, target, load_sem.at[i])
        for i, (source, target) in enumerate(zip(inputs, copied))
    ]
    for load in loads:
        load.start()

    barrier = pltpu.get_barrier_semaphore()
    for d in range(1, groups):
        pl.semaphore_signal(
            barrier, inc=1, device_id=(lax.rem(me + d, groups), tile), device_id_type=MESH
        )
    for other in (left, right):
        pl.semaphore_signal(barrier, inc=1, device_id=(me, other), device_id_type=MESH)

    distances = sorted(range(1, groups), key=lambda d: (abs(2 * d - groups), d))

    def permuted(x):
        return mm(order_ref[...], x).astype(BF16)

    loads[0].wait()
    wants = {}
    for d in distances:
        owner = lax.rem(me + d, groups)
        want = jnp.int32(0)
        for p in range(per_owner):
            second = pairs_ref[1, owner * per_owner + p]
            inside = second - me * held
            want = jnp.where((inside >= 0) & (inside < held), inside, want)
        wants[d] = want

    def slab(d, q):
        return pltpu.make_async_remote_copy(
            src_ref=stage.at[d - 1, q],
            dst_ref=got.at[d - 1, q],
            send_sem=send_sem.at[d - 1, q],
            recv_sem=recv_sem.at[d - 1, q],
            device_id=(lax.rem(me + d, groups), tile),
            device_id_type=MESH,
        )

    def fill(d, q):
        for plane in range(2):
            stage[d - 1, q, plane] = permuted(
                slc_ref[wants[d], plane, :, q * part : (q + 1) * part]
            )

    loads[1].wait()
    loads[2].wait()
    for q in range(CHUNKS):
        fill(distances[0], q)
    pl.semaphore_wait(barrier, groups + 1)
    for q in range(CHUNKS):
        slab(distances[0], q).start()
    for d in distances[1:]:
        for q in range(CHUNKS):
            fill(d, q)
            slab(d, q).start()

    for a in range(held):
        for plane in range(2):
            own[a, plane] = permuted(slc_ref[a, plane])

    for q in range(CHUNKS):
        row = lax.broadcasted_iota(jnp.int32, (2 * part, 2 * width), 0)
        col = lax.broadcasted_iota(jnp.int32, (2 * part, 2 * width), 1)
        plane = jnp.where(row >= part, 1, 0)
        goal = plane * width + q * (part // RG_LOOKS) + (row - plane * part) // RG_LOOKS
        looks_w[q] = jnp.where(goal == col, 1.0 / (AZ_LOOKS * RG_LOOKS), 0.0).astype(BF16)

    def halo_copy(d, side):
        return pltpu.make_async_remote_copy(
            src_ref=planes.at[d - 1],
            dst_ref=halo.at[d - 1, side],
            send_sem=halo_send.at[d - 1, side],
            recv_sem=halo_recv.at[d - 1, side],
            device_id=(me, right if side == 0 else left),
            device_id_type=MESH,
        )

    def multilook(d):
        total = jnp.zeros((held * looks, 2 * width), F32)
        for q in range(CHUNKS):
            slab(d, q).wait_recv()
            at = slice(q * part, (q + 1) * part)
            re = [None] * held
            im = [None] * held
            for l in range(AZ_LOOKS):
                rows = slice(l * looks, (l + 1) * looks)
                br = got[d - 1, q, 0, rows, :].astype(F32)
                bi = got[d - 1, q, 1, rows, :].astype(F32)
                for a in range(held):
                    ar = own[a, 0, rows, at].astype(F32)
                    ai = own[a, 1, rows, at].astype(F32)
                    x = ar * br + ai * bi
                    y = ai * br - ar * bi
                    re[a] = x if l == 0 else re[a] + x
                    im[a] = y if l == 0 else im[a] + y
            both = jnp.concatenate(
                [jnp.concatenate(re, axis=0), jnp.concatenate(im, axis=0)], axis=1
            )
            high, low = split(both)
            total = total + mm(high, looks_w[q]) + mm(low, looks_w[q])
        planes[d - 1] = total

    def columns(x):
        high, low = split(x)
        return mm(jnp.concatenate([high, low, high], axis=1), fwd_ref[...])

    def filter_pairs(d):
        mid = columns(planes[d - 1])
        for side in range(2):
            halo_copy(d, side).wait_recv()
        low_part = columns(halo[d - 1, 0])
        later = jnp.where(tile == tiles - 1, 0.0, halo[d - 1, 1])
        high_part = columns(later)

        def patch(first, second, a):
            rows = slice(a * looks, (a + 1) * looks)
            return jnp.concatenate(
                [first[rows, :span], second[rows, :span], first[rows, span:], second[rows, span:]],
                axis=0,
            )

        blocks = [patch(mid, high_part, a) for a in range(held)]
        blocks += [patch(low_part, mid, a) for a in range(held)]
        high, low = split(jnp.concatenate(blocks, axis=1))
        spec = mm(lines_ref[...], jnp.concatenate([high, low, high], axis=0))
        spec_re, spec_im = spec[:PATCH], spec[PATCH:]
        power = spec_re * spec_re + spec_im * spec_im
        rows3 = power + pltpu.roll(power, 1, 0) + pltpu.roll(power, PATCH - 1, 0)
        stacked = jnp.concatenate(
            [rows3[:, i * span : (i + 1) * span] for i in range(2 * held)], axis=0
        )
        high, low = split(stacked)
        sums = mm(jnp.concatenate([high, low], axis=1), smooth_ref[...])
        weights = []
        for i in range(2 * held):
            block = sums[i * PATCH : (i + 1) * PATCH]
            smoothed = block[:, :span] * (1.0 / 9.0)
            mean = jnp.sum(block[:, span:], axis=0, keepdims=True) * (
                1.0 / (3.0 * PATCH * PATCH)
            )
            relative = smoothed / (mean + 1e-6)
            weight = jnp.sqrt(jnp.sqrt(jnp.maximum(relative, 0.1)))
            if i >= held:
                weight = jnp.where(tile == 0, 0.0, weight)
            weights.append(weight)
        weight = jnp.concatenate(weights, axis=1)
        scaled = jnp.concatenate([weight * spec_re, weight * spec_im], axis=0)
        scaled = jnp.concatenate([scaled[:, : held * span], scaled[:, held * span :]], axis=0)
        high, low = split(scaled)
        back = mm(inv_ref[...], jnp.concatenate([high, low, high], axis=0))
        back = jnp.concatenate(
            [
                jnp.concatenate(
                    [back[:HALF, a * span : (a + 1) * span], back[HALF:, a * span : (a + 1) * span]],
                    axis=1,
                )
                for a in range(held)
            ],
            axis=0,
        )
        high, low = split(back)
        final = mm(jnp.concatenate([high, low, high], axis=1), bwd_ref[...])
        for a in range(held):
            result[(d - 1) * held + a] = final[a * looks : (a + 1) * looks]

    for load in loads[3:]:
        load.wait()

    before = None
    for d in distances:
        multilook(d)
        for side in range(2):
            halo_copy(d, side).start()
        if before is not None:
            filter_pairs(before)
        before = d
    filter_pairs(before)

    for p in range(per_owner):
        first = pairs_ref[0, me * per_owner + p] - me * held
        source = pairs_ref[1, me * per_owner + p] // held
        slot = lax.rem(me - source + groups, groups) - 1
        at = jnp.clip(slot * held + first, 0, (groups - 1) * held - 1)
        lines_out = result[at]
        out_ref[p, 0] = lines_out[:, :width]
        out_ref[p, 1] = lines_out[:, width:]

    for d in distances:
        for q in range(CHUNKS):
            slab(d, q).wait_send()
        for side in range(2):
            halo_copy(d, side).wait_send()


def per_device(groups, tiles, slc_stack, pair_list):
    held, _, lines, samples = slc_stack.shape
    per_owner = pair_list.shape[0] // groups
    looks, width = lines // AZ_LOOKS, samples // RG_LOOKS
    part = samples // CHUNKS
    others = groups - 1
    constants = [jnp.asarray(t) for t in (line_order(lines),) + tables(width)]
    operands = [pair_list.T, slc_stack] + constants
    return pl.pallas_call(
        functools.partial(kernel, groups, tiles, held, per_owner, len(operands)),
        out_shape=jax.ShapeDtypeStruct((per_owner, 2, looks, width), F32),
        in_specs=[pl.BlockSpec(memory_space=pltpu.HBM)] * len(operands),
        out_specs=pl.BlockSpec(memory_space=pltpu.VMEM),
        scratch_shapes=[
            pltpu.SMEM(pair_list.shape[::-1], pair_list.dtype),
            *[pltpu.VMEM(x.shape, x.dtype) for x in operands[1:]],
            pltpu.VMEM((held, 2, lines, samples), BF16),
            pltpu.VMEM((others, CHUNKS, 2, lines, part), BF16),
            pltpu.VMEM((others, CHUNKS, 2, lines, part), BF16),
            pltpu.VMEM((CHUNKS, 2 * part, 2 * width), BF16),
            pltpu.VMEM((others, held * looks, 2 * width), F32),
            pltpu.VMEM((others, 2, held * looks, 2 * width), F32),
            pltpu.VMEM((others * held, looks, 2 * width), F32),
            pltpu.SemaphoreType.DMA((len(operands),)),
            pltpu.SemaphoreType.DMA((others, CHUNKS)),
            pltpu.SemaphoreType.DMA((others, CHUNKS)),
            pltpu.SemaphoreType.DMA((others, 2)),
            pltpu.SemaphoreType.DMA((others, 2)),
        ],
        compiler_params=pltpu.CompilerParams(
            collective_id=0, has_side_effects=True, vmem_limit_bytes=VMEM_LIMIT
        ),
    )(*operands)


def solution(mesh):
    groups, tiles = mesh.shape["acq"], mesh.shape["tile"]
    return jax.shard_map(
        functools.partial(per_device, groups, tiles),
        mesh=mesh,
        in_specs=(P("acq", None, "tile", None), P()),
        out_specs=P("acq", None, "tile", None),
        check_vma=False,
    )
```

```python
import functools

import jax
import jax.numpy as jnp
import ml_dtypes
import numpy as np
from jax import lax
from jax.experimental import pallas as pl
from jax.experimental.pallas import tpu as pltpu
from jax.sharding import PartitionSpec as P

AZ_LOOKS = 4
RG_LOOKS = 16
PATCH = 32
HALF = PATCH // 2
CHUNKS = 2
VMEM_LIMIT = 64 * 2**20 - 2**16
MESH = pl.DeviceIdType.MESH
BF16 = jnp.bfloat16
F32 = jnp.float32


def halves(matrix):
    high = matrix.astype(ml_dtypes.bfloat16)
    low = (matrix - high.astype(np.float64)).astype(ml_dtypes.bfloat16)
    return high, low


def tables(width):
    patches = width // HALF
    index = np.arange(PATCH)
    angle = 2.0 * np.pi * ((index[:, None] * index[None, :]) % PATCH) / PATCH
    cos, sin = np.cos(angle), np.sin(angle)
    taper = np.sin(np.pi * (index + 0.5) / PATCH) ** 2
    span = patches * PATCH
    forward = np.zeros((2 * width, 2 * span))
    backward = np.zeros((2 * span, 2 * width))
    for c in range(patches):
        for j in range(PATCH):
            n = c * HALF + j
            if n >= width:
                continue
            at = slice(c * PATCH, (c + 1) * PATCH)
            im = slice(span + c * PATCH, span + (c + 1) * PATCH)
            forward[n, at] = cos[j]
            forward[n, im] = -sin[j]
            forward[width + n, at] = sin[j]
            forward[width + n, im] = cos[j]
            backward[at, n] = cos[:, j] * taper[j]
            backward[im, n] = -sin[:, j] * taper[j]
            backward[at, width + n] = sin[:, j] * taper[j]
            backward[im, width + n] = cos[:, j] * taper[j]
    lines = np.block([[cos, sin], [-sin, cos]])
    scale = taper / float(PATCH * PATCH)
    inverse = np.block([[cos, -sin], [sin, cos]]) * np.concatenate([scale, scale])[:, None]
    upper = np.concatenate([inverse[:HALF], inverse[PATCH : PATCH + HALF]])
    lower = np.concatenate([inverse[HALF:PATCH], inverse[PATCH + HALF :]])
    inverse = np.concatenate([upper, lower], axis=1)
    ring = np.zeros((PATCH, PATCH))
    for k in range(PATCH):
        for step in (-1, 0, 1):
            ring[(k + step) % PATCH, k] = 1.0
    eye = np.eye(patches)
    smooth = np.concatenate([np.kron(eye, ring), np.kron(eye, np.ones((PATCH, PATCH)))], axis=1)

    fh, fl = halves(forward)
    lh, ll = halves(lines)
    ih, il = halves(inverse)
    bh, bl = halves(backward)
    sh = smooth.astype(ml_dtypes.bfloat16)
    return (
        np.concatenate([fh, fh, fl], axis=0),
        np.concatenate([lh, lh, ll], axis=1),
        np.concatenate([ih, ih, il], axis=1),
        np.concatenate([bh, bh, bl], axis=0),
        np.concatenate([sh, sh], axis=0),
    )


def packed(parts):
    wide = max(x.shape[1] for x in parts)
    starts = np.cumsum([0] + [x.shape[0] for x in parts])
    whole = np.zeros((starts[-1], wide), ml_dtypes.bfloat16)
    for start, x in zip(starts, parts):
        whole[start : start + x.shape[0], : x.shape[1]] = x
    return whole, [(int(start), *x.shape) for start, x in zip(starts, parts)]


def split(x):
    high = x.astype(BF16)
    return high, (x - high.astype(F32)).astype(BF16)


def mm(a, b):
    return jnp.dot(a, b, preferred_element_type=F32)


def kernel(
    groups, tiles, held, per_owner, places, operands,
    *refs,
):
    inputs, (out_ref,), held_in = refs[:operands], refs[operands : operands + 1], refs[operands + 1 :]
    copied, rest = held_in[:operands], held_in[operands:]
    pairs_ref, slc_ref, tables_ref = copied
    fwd_ref, lines_ref, inv_ref, bwd_ref, smooth_ref = [
        tables_ref.at[start : start + rows, :columns] for start, rows, columns in places
    ]
    (own, stage, got, looks_w, planes, halo, result,
     load_sem, send_sem, recv_sem, halo_send, halo_recv) = rest
    me = lax.axis_index("acq")
    tile = lax.axis_index("tile")
    lines = slc_ref.shape[2]
    samples = slc_ref.shape[3]
    looks = lines // AZ_LOOKS
    width = samples // RG_LOOKS
    part = samples // CHUNKS
    span = (width // HALF) * PATCH
    left = lax.rem(tile + tiles - 1, tiles)
    right = lax.rem(tile + 1, tiles)

    loads = [
        pltpu.make_async_copy(source, target, load_sem.at[i])
        for i, (source, target) in enumerate(zip(inputs, copied))
    ]
    for load in loads:
        load.start()

    barrier = pltpu.get_barrier_semaphore()
    for d in range(1, groups):
        pl.semaphore_signal(
            barrier, inc=1, device_id=(lax.rem(me + d, groups), tile), device_id_type=MESH
        )
    for other in (left, right):
        pl.semaphore_signal(barrier, inc=1, device_id=(me, other), device_id_type=MESH)

    distances = sorted(range(1, groups), key=lambda d: (abs(2 * d - groups), d))

    row = lax.broadcasted_iota(jnp.int32, (lines, lines), 0)
    col = lax.broadcasted_iota(jnp.int32, (lines, lines), 1)
    origin = (row % looks) * AZ_LOOKS + row // looks
    order = jnp.where(origin == col, 1.0, 0.0).astype(BF16)

    def permuted(x):
        return mm(order, x).astype(BF16)

    loads[0].wait()
    wants = {}
    for d in distances:
        owner = lax.rem(me + d, groups)
        want = jnp.int32(0)
        for p in range(per_owner):
            second = pairs_ref[1, owner * per_owner + p]
            inside = second - me * held
            want = jnp.where((inside >= 0) & (inside < held), inside, want)
        wants[d] = want

    def slab(d, q):
        return pltpu.make_async_remote_copy(
            src_ref=stage.at[d - 1, q],
            dst_ref=got.at[d - 1, q],
            send_sem=send_sem.at[d - 1, q],
            recv_sem=recv_sem.at[d - 1, q],
            device_id=(lax.rem(me + d, groups), tile),
            device_id_type=MESH,
        )

    def fill(d, q):
        for plane in range(2):
            stage[d - 1, q, plane] = permuted(
                slc_ref[wants[d], plane, :, q * part : (q + 1) * part]
            )

    loads[1].wait()
    for q in range(CHUNKS):
        fill(distances[0], q)
    pl.semaphore_wait(barrier, groups + 1)
    for q in range(CHUNKS):
        slab(distances[0], q).start()
    for d in distances[1:]:
        for q in range(CHUNKS):
            fill(d, q)
            slab(d, q).start()

    for a in range(held):
        for plane in range(2):
            own[a, plane] = permuted(slc_ref[a, plane])

    for q in range(CHUNKS):
        row = lax.broadcasted_iota(jnp.int32, (2 * part, 2 * width), 0)
        col = lax.broadcasted_iota(jnp.int32, (2 * part, 2 * width), 1)
        plane = jnp.where(row >= part, 1, 0)
        goal = plane * width + q * (part // RG_LOOKS) + (row - plane * part) // RG_LOOKS
        looks_w[q] = jnp.where(goal == col, 1.0 / (AZ_LOOKS * RG_LOOKS), 0.0).astype(BF16)

    def halo_copy(d, side):
        return pltpu.make_async_remote_copy(
            src_ref=planes.at[d - 1],
            dst_ref=halo.at[d - 1, side],
            send_sem=halo_send.at[d - 1, side],
            recv_sem=halo_recv.at[d - 1, side],
            device_id=(me, right if side == 0 else left),
            device_id_type=MESH,
        )

    def multilook(d):
        total = jnp.zeros((held * looks, 2 * width), F32)
        for q in range(CHUNKS):
            slab(d, q).wait_recv()
            at = slice(q * part, (q + 1) * part)
            re = [None] * held
            im = [None] * held
            for l in range(AZ_LOOKS):
                rows = slice(l * looks, (l + 1) * looks)
                br = got[d - 1, q, 0, rows, :].astype(F32)
                bi = got[d - 1, q, 1, rows, :].astype(F32)
                for a in range(held):
                    ar = own[a, 0, rows, at].astype(F32)
                    ai = own[a, 1, rows, at].astype(F32)
                    x = ar * br + ai * bi
                    y = ai * br - ar * bi
                    re[a] = x if l == 0 else re[a] + x
                    im[a] = y if l == 0 else im[a] + y
            both = jnp.concatenate(
                [jnp.concatenate(re, axis=0), jnp.concatenate(im, axis=0)], axis=1
            )
            high, low = split(both)
            total = total + mm(high, looks_w[q]) + mm(low, looks_w[q])
        planes[d - 1] = total

    def columns(x):
        high, low = split(x)
        return mm(jnp.concatenate([high, low, high], axis=1), fwd_ref[...])

    def filter_pairs(d):
        mid = columns(planes[d - 1])
        for side in range(2):
            halo_copy(d, side).wait_recv()
        low_part = columns(halo[d - 1, 0])
        later = jnp.where(tile == tiles - 1, 0.0, halo[d - 1, 1])
        high_part = columns(later)

        def patch(first, second, a):
            rows = slice(a * looks, (a + 1) * looks)
            return jnp.concatenate(
                [first[rows, :span], second[rows, :span], first[rows, span:], second[rows, span:]],
                axis=0,
            )

        blocks = [patch(mid, high_part, a) for a in range(held)]
        blocks += [patch(low_part, mid, a) for a in range(held)]
        high, low = split(jnp.concatenate(blocks, axis=1))
        spec = mm(lines_ref[...], jnp.concatenate([high, low, high], axis=0))
        spec_re, spec_im = spec[:PATCH], spec[PATCH:]
        power = spec_re * spec_re + spec_im * spec_im
        rows3 = power + pltpu.roll(power, 1, 0) + pltpu.roll(power, PATCH - 1, 0)
        stacked = jnp.concatenate(
            [rows3[:, i * span : (i + 1) * span] for i in range(2 * held)], axis=0
        )
        high, low = split(stacked)
        sums = mm(jnp.concatenate([high, low], axis=1), smooth_ref[...])
        weights = []
        for i in range(2 * held):
            block = sums[i * PATCH : (i + 1) * PATCH]
            smoothed = block[:, :span] * (1.0 / 9.0)
            mean = jnp.sum(block[:, span:], axis=0, keepdims=True) * (
                1.0 / (3.0 * PATCH * PATCH)
            )
            relative = smoothed / (mean + 1e-6)
            weight = jnp.sqrt(jnp.sqrt(jnp.maximum(relative, 0.1)))
            if i >= held:
                weight = jnp.where(tile == 0, 0.0, weight)
            weights.append(weight)
        weight = jnp.concatenate(weights, axis=1)
        scaled = jnp.concatenate([weight * spec_re, weight * spec_im], axis=0)
        scaled = jnp.concatenate([scaled[:, : held * span], scaled[:, held * span :]], axis=0)
        high, low = split(scaled)
        back = mm(inv_ref[...], jnp.concatenate([high, low, high], axis=0))
        back = jnp.concatenate(
            [
                jnp.concatenate(
                    [back[:HALF, a * span : (a + 1) * span], back[HALF:, a * span : (a + 1) * span]],
                    axis=1,
                )
                for a in range(held)
            ],
            axis=0,
        )
        high, low = split(back)
        final = mm(jnp.concatenate([high, low, high], axis=1), bwd_ref[...])
        for a in range(held):
            result[(d - 1) * held + a] = final[a * looks : (a + 1) * looks]

    for load in loads[2:]:
        load.wait()

    for d in distances:
        multilook(d)
        for side in range(2):
            halo_copy(d, side).start()
    for d in distances:
        filter_pairs(d)

    for p in range(per_owner):
        first = pairs_ref[0, me * per_owner + p] - me * held
        source = pairs_ref[1, me * per_owner + p] // held
        slot = lax.rem(me - source + groups, groups) - 1
        at = jnp.clip(slot * held + first, 0, (groups - 1) * held - 1)
        lines_out = result[at]
        out_ref[p, 0] = lines_out[:, :width]
        out_ref[p, 1] = lines_out[:, width:]

    for d in distances:
        for q in range(CHUNKS):
            slab(d, q).wait_send()
        for side in range(2):
            halo_copy(d, side).wait_send()


def per_device(groups, tiles, slc_stack, pair_list):
    held, _, lines, samples = slc_stack.shape
    per_owner = pair_list.shape[0] // groups
    looks, width = lines // AZ_LOOKS, samples // RG_LOOKS
    part = samples // CHUNKS
    others = groups - 1
    constants, places = packed(tables(width))
    operands = [pair_list.T, slc_stack, jnp.asarray(constants)]
    return pl.pallas_call(
        functools.partial(kernel, groups, tiles, held, per_owner, places, len(operands)),
        out_shape=jax.ShapeDtypeStruct((per_owner, 2, looks, width), F32),
        in_specs=[pl.BlockSpec(memory_space=pltpu.HBM)] * len(operands),
        out_specs=pl.BlockSpec(memory_space=pltpu.VMEM),
        scratch_shapes=[
            pltpu.SMEM(pair_list.shape[::-1], pair_list.dtype),
            *[pltpu.VMEM(x.shape, x.dtype) for x in operands[1:]],
            pltpu.VMEM((held, 2, lines, samples), BF16),
            pltpu.VMEM((others, CHUNKS, 2, lines, part), BF16),
            pltpu.VMEM((others, CHUNKS, 2, lines, part), BF16),
            pltpu.VMEM((CHUNKS, 2 * part, 2 * width), BF16),
            pltpu.VMEM((others, held * looks, 2 * width), F32),
            pltpu.VMEM((others, 2, held * looks, 2 * width), F32),
            pltpu.VMEM((others * held, looks, 2 * width), F32),
            pltpu.SemaphoreType.DMA((len(operands),)),
            pltpu.SemaphoreType.DMA((others, CHUNKS)),
            pltpu.SemaphoreType.DMA((others, CHUNKS)),
            pltpu.SemaphoreType.DMA((others, 2)),
            pltpu.SemaphoreType.DMA((others, 2)),
        ],
        compiler_params=pltpu.CompilerParams(
            collective_id=0, has_side_effects=True, vmem_limit_bytes=VMEM_LIMIT
        ),
    )(*operands)


def solution(mesh):
    groups, tiles = mesh.shape["acq"], mesh.shape["tile"]
    return jax.shard_map(
        functools.partial(per_device, groups, tiles),
        mesh=mesh,
        in_specs=(P("acq", None, "tile", None), P()),
        out_specs=P("acq", None, "tile", None),
        check_vma=False,
    )
```
